32 devices in a mesh: section: 4 (over x, core), dp: 8 (over z, y).
Axes of the slice: x: 2, y: 2, z: 4, core: 2. Of those that a mesh axis runs over, the one named last changes fastest.
Arguments:
- layer_input: bfloat16 [4, 2, 2048, 4096], P('section', None, 'dp'), may hold values from -6 to 6
- queries: bfloat16 [4, 2, 2048, 4096], P('section', None, 'dp'), may hold values from -85 to 85
- attn_grad: bfloat16 [4, 2, 2048, 4096], P('section', None, 'dp'), may hold values from -6 to 6
- top_grad: bfloat16 [2, 2048, 4096], P(None, 'dp', 'section'), may hold values from -6 to 6
- positions: int32 [2, 2048], P(None, 'dp'), may hold values from 0 to 255, as said below
- norm_gain: float32 [4, 4096], P('section'), may hold values from 0.1 to 1.9
- key_weight: bfloat16 [4, 4096, 512], P('section'), may hold values from -0.09375 to 0.09375
- value_weight: bfloat16 [4, 4096, 512], P('section'), may hold values from -0.09375 to 0.09375
Outputs:
- passed_grad: bfloat16 [4, 2, 2048, 4096], P('section', None, 'dp')
- key_grad: float32 [4, 4096, 512], P('section', 'dp')
- value_grad: float32 [4, 4096, 512], P('section', 'dp')
- gain_grad: float32 [4, 4096], P('section', 'dp')
The draws below stay inside these ranges and needn't reach their ends.
Inputs may be any that keep to these rules, and one draw needn't show every extreme that they name: `positions`: within each block of 256 tokens the first position is 0; each later position is 0 (a new document) or one more than the previous one. In each micro-batch the first block of 256 tokens is a single document.
All inputs are finite; a program needn't handle non-finite values.
Results may differ from the reference program's by a relative error of at most 0.0095.
The reference program's roundings to bfloat16 on the way (of `normed`, `probs_b`, `dscores`, `dkeys` and `dvalues`) count: a program that leaves them out, or rounds other values in their place, can miss the bound.
Values may be sent and summed in bfloat16 or wider, within the bound.
A program may use at most 192 MiB of HBM per device.

```python
import jax
import jax.numpy as jnp
from jax import lax

D = 4096
HD = 128
KV = 4
GRP = 8
MB = 2
SEQ = 256
HQ = 32
KVW = 512
QW = 4096
SECTIONS = 4
TOKENS = 2048
SEQS = 16
N_DP = 8


def draw_queries(key, part):
    first_key = jax.random.fold_in(key, 0)
    shape = (SECTIONS, MB, TOKENS, HQ, HD)
    values_f = jnp.clip(jax.random.normal(first_key, shape, jnp.float32), -6.0, 6.0)
    return values_f.reshape(SECTIONS, MB, TOKENS, HQ * HD).astype(jnp.bfloat16)


def draw_positions(key, part):
    rolled = jax.random.randint(key, (MB, TOKENS), 0, 48)
    index = jnp.arange(TOKENS, dtype=jnp.int32)
    first = index % SEQ == 0
    later_block = index >= SEQ
    is_start = (rolled == 0) & later_block[None, :] | first[None, :]
    start_at = jnp.where(is_start, index[None, :], jnp.zeros((MB, TOKENS), jnp.int32))
    latest = lax.cummax(start_at, axis=1)
    return (index[None, :] - latest).astype(jnp.int32)


def spiked(entries, stream_key, source, target, parts, factor):
    owner, partner = [(jnp.arange(entries.shape[axis_at]) // (entries.shape[axis_at] // parts)).reshape([-1 if axis == axis_at else 1 for axis in range(entries.ndim)]) for axis_at in (source, target)]
    chosen = jax.random.permutation(stream_key, parts)[partner]
    strong = (owner == chosen) | (owner == (partner + parts // 2) % parts)
    return jnp.where(strong, factor * entries, entries)


def shard_levels(rng, shape, cuts, smallest, largest):
    loudness = 1.0
    for dim, blocks in cuts:
        draws = jax.random.uniform(jax.random.fold_in(jax.random.fold_in(rng, 6), dim), (blocks,), jnp.float32, smallest / len(cuts), largest / len(cuts))
        loudness = loudness * jnp.repeat(jnp.exp(draws), shape[dim] // blocks).reshape((-1,) + (1,) * (len(shape) - 1 - dim))
    return loudness


def noise(key, extent, scale, limit, cuts=(), kind=jnp.bfloat16):
    gain = shard_levels(key, extent, cuts, -0.22, 0.18) if cuts else 1.0
    entries = jax.random.normal(key, extent, jnp.float32) * scale * gain
    return jnp.minimum(jnp.maximum(entries, -limit), limit).astype(kind)


def heavy_noise(own_key, extent, deviation, most, cuts, heavy, kind=jnp.bfloat16):
    drawn = deviation * jax.random.normal(own_key, extent, jnp.float32)
    if cuts:
        drawn = drawn * shard_levels(own_key, extent, cuts, -0.22, 0.18)
    return jnp.clip(spiked(drawn, jax.random.fold_in(own_key, 3), *heavy), -most, most).astype(kind)


def setup_inputs(seed: int = 0) -> dict:
    streams_of = jax.random.split(jax.random.key(seed), 9)
    return {
        "layer_input": heavy_noise(streams_of[0], (SECTIONS, MB, TOKENS, D), 1.0, 6.0, ((0, 4), (2, 8)), (2, 3, 8, 2.0)),
        "queries": draw_queries(jax.random.fold_in(streams_of[8], 71), 0),
        "attn_grad": noise(streams_of[2], (SECTIONS, MB, TOKENS, QW), 1.0, 6.0, ((0, 4), (2, 8))),
        "top_grad": noise(streams_of[3], (MB, TOKENS, D), 1.0, 6.0, ((1, 8), (2, 4))),
        "positions": draw_positions(jax.random.fold_in(streams_of[8], 71), 0),
        "norm_gain": jnp.clip(1.0 + 0.18 * jax.random.normal(streams_of[5], (SECTIONS, D), jnp.float32), 0.1, 1.9),
        "key_weight": noise(streams_of[6], (SECTIONS, D, KVW), D ** -0.5, 0.09375, ((0, 4),)),
        "value_weight": noise(streams_of[7], (SECTIONS, D, KVW), D ** -0.5, 0.09375, ((0, 4),)),
    }


EPS = 1e-05

def section_terms(hidden_rows, query_rows, grad_rows, places, gain_row, w_key, w_value):
    count_seq, length, width = hidden_rows.shape
    values_f = hidden_rows.astype(jnp.float32)
    inverse = lax.rsqrt(lax.optimization_barrier(jnp.mean(values_f * values_f, axis=-1, keepdims=True)) + EPS)
    unit_rows = values_f * inverse
    normed = (unit_rows * gain_row).astype(jnp.bfloat16)
    flat = normed.reshape(count_seq * length, width)
    key_flat = jnp.dot(flat, w_key, preferred_element_type=jnp.float32).astype(jnp.bfloat16)
    value_flat = jnp.dot(flat, w_value, preferred_element_type=jnp.float32).astype(jnp.bfloat16)
    key_heads = key_flat.reshape(count_seq, length, KV, HD).astype(jnp.float32)
    value_heads = value_flat.reshape(count_seq, length, KV, HD).astype(jnp.float32)
    query_heads = query_rows.reshape(count_seq, length, KV, GRP, HD).astype(jnp.float32)
    grad_heads = grad_rows.reshape(count_seq, length, KV, GRP, HD).astype(jnp.float32)
    score_scale = HD ** (-0.5)
    scores = jnp.einsum('bqgjd,bkgd->bgjqk', query_heads, key_heads) * score_scale
    position = jnp.arange(length, dtype=jnp.int32)
    distance = position[None, :, None] - position[None, None, :]
    allowed = (distance >= 0) & (distance <= places[:, :, None])
    scores = jnp.where(allowed[:, None, None], scores, jnp.float32(-1e+30))
    probs = jax.nn.softmax(scores, axis=-1)
    probs_b = probs.astype(jnp.bfloat16).astype(jnp.float32)
    dprobs = jnp.einsum('bqgjd,bkgd->bgjqk', grad_heads, value_heads)
    row_total = lax.optimization_barrier(jnp.sum(probs * dprobs, axis=-1, keepdims=True))
    dscores = (probs * (dprobs - row_total)).astype(jnp.bfloat16).astype(jnp.float32)
    dkeys = (jnp.einsum('bgjqk,bqgjd->bkgd', dscores, query_heads) * score_scale).astype(jnp.bfloat16)
    dvalues = jnp.einsum('bgjqk,bqgjd->bkgd', probs_b, grad_heads).astype(jnp.bfloat16)
    dkeys = dkeys.reshape(count_seq * length, KV * HD)
    dvalues = dvalues.reshape(count_seq * length, KV * HD)
    dnormed = jnp.dot(dkeys, w_key.T, preferred_element_type=jnp.float32) + jnp.dot(dvalues, w_value.T, preferred_element_type=jnp.float32)
    unit_flat = unit_rows.reshape(count_seq * length, width)
    inverse_flat = inverse.reshape(count_seq * length, 1)
    gain_term = lax.optimization_barrier(jnp.sum(dnormed * unit_flat, axis=0))
    dunit = dnormed * gain_row
    branch = inverse_flat * (dunit - unit_flat * lax.optimization_barrier(jnp.mean(dunit * unit_flat, axis=-1, keepdims=True)))
    key_term = jnp.dot(flat.T, dkeys, preferred_element_type=jnp.float32)
    value_term = jnp.dot(flat.T, dvalues, preferred_element_type=jnp.float32)
    return (branch.reshape(count_seq * length, width), key_term, value_term, gain_term)

def reference(layer_input, queries, attn_grad, top_grad, positions, norm_gain, key_weight, value_weight):
    branch_all = []
    key_out = []
    value_out = []
    gain_out = []
    for section_index in range(SECTIONS):
        branch_mb = []
        key_sum = jnp.zeros((D, KVW), jnp.float32)
        value_sum = jnp.zeros((D, KVW), jnp.float32)
        gain_sum = jnp.zeros((D,), jnp.float32)
        for micro_index in range(MB):
            hidden_rows = layer_input[section_index, micro_index].reshape(N_DP, SEQ, D)
            query_rows = queries[section_index, micro_index].reshape(N_DP, SEQ, QW)
            grad_rows = attn_grad[section_index, micro_index].reshape(N_DP, SEQ, QW)
            places = positions[micro_index].reshape(N_DP, SEQ)
            branch, key_term, value_term, gain_term = section_terms(hidden_rows, query_rows, grad_rows, places, norm_gain[section_index], key_weight[section_index], value_weight[section_index])
            branch_mb.append(branch)
            key_sum = key_sum + key_term
            value_sum = value_sum + value_term
            gain_sum = gain_sum + gain_term
        branch_all.append(jnp.stack(branch_mb))
        key_out.append(key_sum / SEQS)
        value_out.append(value_sum / SEQS)
        gain_out.append(gain_sum / SEQS)
    running = top_grad
    passed = [None] * SECTIONS
    for section_index in range(SECTIONS - 1, -1, -1):
        running = (running.astype(jnp.float32) + branch_all[section_index]).astype(jnp.bfloat16)
        passed[section_index] = running
    return (jnp.stack(passed), jnp.stack(key_out), jnp.stack(value_out), jnp.stack(gain_out))
```

```python
import functools

import jax
import jax.numpy as jnp
from jax import lax
from jax.experimental import pallas as pl
from jax.experimental.pallas import tpu as pltpu
from jax.sharding import PartitionSpec as P

HD = 128
GRP = 8
EPS = 1e-05
PAD = 16
LOG2E = 1.4426950408889634
VMEM = 50 * 1024 * 1024
NT = (((1,), (1,)), ((), ()))
TN = (((0,), (0,)), ((), ()))


def attention_body(k_ref, v_ref, q_ref, g_ref, pos_ref, out_ref):
    length = k_ref.shape[0]
    scale = HD ** (-0.5)
    keys, values = k_ref[...], v_ref[...]
    key_at = lax.broadcasted_iota(jnp.int32, (length, length), 0)
    query_at = lax.broadcasted_iota(jnp.int32, (length, length), 1)
    distance = query_at - key_at
    allowed = (distance >= 0) & (distance <= pos_ref[0])
    dkeys = jnp.zeros((length, HD), jnp.float32)
    dvalues = jnp.zeros((length, HD), jnp.float32)
    for head in range(GRP):
        columns = slice(head * HD, (head + 1) * HD)
        query, grad = q_ref[0, :, columns], g_ref[0, :, columns]
        scores = lax.dot_general(keys, query, NT, preferred_element_type=jnp.float32)
        scores = jnp.where(allowed, scores, -1e30)
        top = jnp.max(scores, axis=0, keepdims=True)
        raw = jnp.exp2((scores - top) * (scale * LOG2E))
        probs = raw * (1.0 / jnp.sum(raw, axis=0, keepdims=True))
        dprobs = lax.dot_general(values, grad, NT, preferred_element_type=jnp.float32)
        total = jnp.sum(probs * dprobs, axis=0, keepdims=True)
        dscores = (probs * (dprobs - total)).astype(jnp.bfloat16)
        dkeys += jnp.dot(dscores, query, preferred_element_type=jnp.float32)
        dvalues += jnp.dot(probs.astype(jnp.bfloat16), grad, preferred_element_type=jnp.float32)
    out_ref[0] = (dkeys * scale).astype(jnp.bfloat16)
    out_ref[1] = dvalues.astype(jnp.bfloat16)


def attention_grads(keys, values, queries, grads, places, first, count):
    micro, length, _ = queries.shape
    wide = GRP * HD
    return pl.pallas_call(
        attention_body,
        grid=(count, micro),
        in_specs=[
            pl.BlockSpec((length, HD), lambda g, m: (m, first + g)),
            pl.BlockSpec((length, HD), lambda g, m: (m, first + g)),
            pl.BlockSpec((1, length, wide), lambda g, m: (m, 0, first + g)),
            pl.BlockSpec((1, length, wide), lambda g, m: (m, 0, first + g)),
            pl.BlockSpec((1, 1, length), lambda g, m: (m, 0, 0)),
        ],
        out_specs=pl.BlockSpec((2, length, HD), lambda g, m: (0, m, g)),
        out_shape=jax.ShapeDtypeStruct((2, micro * length, count * HD), jnp.bfloat16),
        cost_estimate=pl.CostEstimate(
            flops=8 * count * micro * GRP * length * length * HD,
            bytes_accessed=4 * count * micro * length * wide,
            transcendentals=count * micro * GRP * length * length,
        ),
        compiler_params=pltpu.CompilerParams(vmem_limit_bytes=VMEM),
        name="attention_grads",
    )(keys, values, queries, grads, places)


def weight_body(own_ref, other_ref, own_d_ref, other_d_ref, out_ref):
    rows = own_ref.shape[1]
    own_d = jnp.concatenate([own_d_ref[0], own_d_ref[1]], axis=1)
    other_d = jnp.concatenate([other_d_ref[0], other_d_ref[1]], axis=1)
    total = lax.dot_general(own_ref[...], own_d, TN, preferred_element_type=jnp.float32)
    total += lax.dot_general(other_ref[...], other_d, TN, preferred_element_type=jnp.float32)
    most = jnp.maximum(jnp.max(jnp.abs(total), axis=0, keepdims=True), 1e-30)
    power = jnp.ceil(jnp.log2(most * (1.0 / 32000.0)))
    coded = jnp.round(total * jnp.exp2(-power)).astype(jnp.int32)
    out_ref[0, :rows] = coded.astype(jnp.int16)
    tail = jnp.broadcast_to(power.astype(jnp.int32), (PAD, power.shape[1]))
    out_ref[0, rows:] = tail.astype(jnp.int16)


def weight_terms(own, other, own_d, other_d, chunks):
    tokens, width = own.shape
    rows = width // chunks
    columns = 2 * own_d.shape[2]
    block = pl.BlockSpec((tokens, rows), lambda k: (0, k))
    whole = pl.BlockSpec(own_d.shape, lambda k: (0, 0, 0))
    return pl.pallas_call(
        weight_body,
        grid=(chunks,),
        in_specs=[block, block, whole, whole],
        out_specs=pl.BlockSpec((1, rows + PAD, columns), lambda k: (k, 0, 0)),
        out_shape=jax.ShapeDtypeStruct((chunks, rows + PAD, columns), jnp.int16),
        cost_estimate=pl.CostEstimate(
            flops=4 * tokens * width * columns,
            bytes_accessed=4 * tokens * width + 2 * width * columns,
            transcendentals=0,
        ),
        compiler_params=pltpu.CompilerParams(vmem_limit_bytes=VMEM),
        name="weight_terms",
    )(own, other, own_d, other_d)


def branch_body(x_ref, low_ref, high_ref, wk_ref, wv_ref, gain_ref, out_ref, term_ref):
    width = x_ref.shape[1]
    dk = jnp.concatenate([low_ref[0], high_ref[0]], axis=1)
    dv = jnp.concatenate([low_ref[1], high_ref[1]], axis=1)
    dnormed = lax.dot_general(dk, wk_ref[...], NT, preferred_element_type=jnp.float32)
    dnormed += lax.dot_general(dv, wv_ref[...], NT, preferred_element_type=jnp.float32)
    x = x_ref[...].astype(jnp.float32)
    inverse = lax.rsqrt(jnp.sum(x * x, axis=-1, keepdims=True) * (1.0 / width) + EPS)
    unit = x * inverse
    product = dnormed * unit
    term = jnp.sum(product, axis=0, keepdims=True)
    first = pl.program_id(0) == 0

    @pl.when(first)
    def _():
        term_ref[...] = term

    @pl.when(jnp.logical_not(first))
    def _():
        term_ref[...] += term

    gain = gain_ref[...]
    mean = jnp.sum(product * gain, axis=-1, keepdims=True) * (1.0 / width)
    out_ref[...] = inverse * (dnormed * gain - unit * mean)


def branch_terms(x, low, high, wk, wv, gain):
    tokens, width = x.shape
    rows = 128
    half = low.shape[2]
    weight = pl.BlockSpec(wk.shape, lambda i: (0, 0))
    return pl.pallas_call(
        branch_body,
        grid=(tokens // rows,),
        in_specs=[
            pl.BlockSpec((rows, width), lambda i: (i, 0)),
            pl.BlockSpec((2, rows, half), lambda i: (0, i, 0)),
            pl.BlockSpec((2, rows, half), lambda i: (0, i, 0)),
            weight,
            weight,
            pl.BlockSpec((1, width), lambda i: (0, 0)),
        ],
        out_specs=[
            pl.BlockSpec((rows, width), lambda i: (i, 0)),
            pl.BlockSpec((1, width), lambda i: (0, 0)),
        ],
        out_shape=[
            jax.ShapeDtypeStruct((tokens, width), jnp.float32),
            jax.ShapeDtypeStruct((1, width), jnp.float32),
        ],
        cost_estimate=pl.CostEstimate(
            flops=4 * tokens * width * wk.shape[1],
            bytes_accessed=6 * tokens * width + 4 * width * wk.shape[1],
            transcendentals=0,
        ),
        compiler_params=pltpu.CompilerParams(vmem_limit_bytes=VMEM),
        name="branch_terms",
    )(x, low, high, wk, wv, gain)


def shards(
    layer_input, queries, attn_grad, top_grad, positions, norm_gain, key_weight, value_weight
):
    _, micro, length, width = layer_input.shape
    tokens = micro * length
    replicas = lax.axis_size("dp")
    chunks = replicas // 2
    rows = width // replicas
    seq_total = micro * replicas
    me = lax.axis_index("dp")
    side = lax.rem(me, 2)
    place = me // 2
    swap = [(i, i ^ 1) for i in range(replicas)]
    wk, wv = key_weight[0], value_weight[0]
    x = layer_input[0].reshape(tokens, width)
    top_full = lax.all_gather(top_grad, "section", axis=2, tiled=True)

    def parity(values, which):
        parts = []
        for k in range(chunks):
            owner = lax.rem(place + k, chunks) * 2 + which
            parts.append(lax.dynamic_slice_in_dim(values, owner * rows, rows, values.ndim - 1))
        return jnp.concatenate(parts, axis=-1)

    x_f = x.astype(jnp.float32)
    inverse = lax.rsqrt(jnp.mean(x_f * x_f, axis=-1, keepdims=True) + EPS)
    normed = (x_f * inverse * norm_gain).astype(jnp.bfloat16)
    other = lax.ppermute(parity(normed, 1 - side), "dp", swap)
    own = parity(normed, side)
    keys = jnp.dot(normed, wk, preferred_element_type=jnp.float32).astype(jnp.bfloat16)
    values = jnp.dot(normed, wv, preferred_element_type=jnp.float32).astype(jnp.bfloat16)

    heads = keys.shape[1] // HD
    half = heads // 2
    places = positions.reshape(micro, 1, length)
    grads, sums = [], []

    def shift_from(k):
        pairs = []
        for i in range(replicas):
            target = ((i // 2 + k) % chunks) * 2 + i % 2
            pairs.append((i, target))
        return pairs

    for first in (0, half):
        mine = attention_grads(keys, values, queries[0], attn_grad[0], places, first, half)
        grads.append(mine)
        theirs = lax.ppermute(mine, "dp", swap)
        coded = weight_terms(own, other, mine, theirs, chunks)
        pieces = [coded[0]]
        for k in range(1, chunks):
            pieces.append(lax.ppermute(coded[k], "dp", shift_from(k)))
        sums.append(pieces)

    branch, term = branch_terms(x, grads[0], grads[1], wk, wv, norm_gain)

    gain_part = parity(term, side) + lax.ppermute(parity(term, 1 - side), "dp", swap)
    gain_share = gain_part[:, :rows]
    for k in range(1, chunks):
        piece = gain_part[:, k * rows : (k + 1) * rows]
        gain_share = gain_share + lax.ppermute(piece, "dp", shift_from(k))
    gain_share = gain_share / seq_total

    sections = lax.axis_size("section")
    section = lax.axis_index("section")
    passed = []
    for m in range(micro):
        mine = branch[m * length : (m + 1) * length]
        current = (top_full[m].astype(jnp.float32) + mine).astype(jnp.bfloat16)
        for s in range(sections - 2, -1, -1):
            came = lax.ppermute(current, "section", [(s + 1, s)])
            added = (came.astype(jnp.float32) + mine).astype(jnp.bfloat16)
            current = jnp.where(section == s, added, current)
        passed.append(current)
    passed = jnp.stack(passed)

    def decoded(pieces):
        total = None
        for piece in pieces:
            unit = jnp.exp2(piece[rows : rows + 1].astype(jnp.float32))
            part = piece[:rows].astype(jnp.float32) * unit
            total = part if total is None else total + part
        return total / seq_total

    low, high = decoded(sums[0]), decoded(sums[1])
    wide = half * HD
    key_share = jnp.concatenate([low[:, :wide], high[:, :wide]], axis=1)
    value_share = jnp.concatenate([low[:, wide:], high[:, wide:]], axis=1)
    return (passed[None], key_share[None], value_share[None], gain_share)


def solution(mesh):
    return jax.shard_map(
        shards,
        mesh=mesh,
        in_specs=(
            P("section", None, "dp", None),
            P("section", None, "dp", None),
            P("section", None, "dp", None),
            P(None, "dp", "section"),
            P(None, "dp"),
            P("section", None),
            P("section", None, None),
            P("section", None, None),
        ),
        out_specs=(
            P("section", None, "dp", None),
            P("section", "dp", None),
            P("section", "dp", None),
            P("section", "dp"),
        ),
        check_vma=False,
    )
```

```python
import functools

import jax
import jax.numpy as jnp
from jax import lax
from jax.experimental import pallas as pl
from jax.experimental.pallas import tpu as pltpu
from jax.sharding import PartitionSpec as P

HD = 128
GRP = 8
EPS = 1e-05
PAD = 16
LOG2E = 1.4426950408889634
VMEM = 50 * 1024 * 1024
NT = (((1,), (1,)), ((), ()))
TN = (((0,), (0,)), ((), ()))


def attention_body(k_ref, v_ref, q_ref, g_ref, pos_ref, out_ref):
    length = k_ref.shape[0]
    scale = HD ** (-0.5)
    keys, values = k_ref[...], v_ref[...]
    key_at = lax.broadcasted_iota(jnp.int32, (length, length), 0)
    query_at = lax.broadcasted_iota(jnp.int32, (length, length), 1)
    distance = query_at - key_at
    allowed = (distance >= 0) & (distance <= pos_ref[0])
    dkeys = jnp.zeros((length, HD), jnp.float32)
    dvalues = jnp.zeros((length, HD), jnp.float32)
    for head in range(GRP):
        columns = slice(head * HD, (head + 1) * HD)
        query, grad = q_ref[0, :, columns], g_ref[0, :, columns]
        scores = lax.dot_general(keys, query, NT, preferred_element_type=jnp.float32)
        scores = jnp.where(allowed, scores, -1e30)
        top = jnp.max(scores, axis=0, keepdims=True)
        raw = jnp.exp2((scores - top) * (scale * LOG2E))
        probs = raw * (1.0 / jnp.sum(raw, axis=0, keepdims=True))
        dprobs = lax.dot_general(values, grad, NT, preferred_element_type=jnp.float32)
        total = jnp.sum(probs * dprobs, axis=0, keepdims=True)
        dscores = (probs * (dprobs - total)).astype(jnp.bfloat16)
        dkeys += jnp.dot(dscores, query, preferred_element_type=jnp.float32)
        dvalues += jnp.dot(probs.astype(jnp.bfloat16), grad, preferred_element_type=jnp.float32)
    out_ref[0] = (dkeys * scale).astype(jnp.bfloat16)
    out_ref[1] = dvalues.astype(jnp.bfloat16)


def attention_grads(keys, values, queries, grads, places, first, count):
    micro, length, _ = queries.shape
    wide = GRP * HD
    return pl.pallas_call(
        attention_body,
        grid=(count, micro),
        in_specs=[
            pl.BlockSpec((length, HD), lambda g, m: (m, first + g)),
            pl.BlockSpec((length, HD), lambda g, m: (m, first + g)),
            pl.BlockSpec((1, length, wide), lambda g, m: (m, 0, first + g)),
            pl.BlockSpec((1, length, wide), lambda g, m: (m, 0, first + g)),
            pl.BlockSpec((1, 1, length), lambda g, m: (m, 0, 0)),
        ],
        out_specs=pl.BlockSpec((2, length, HD), lambda g, m: (0, m, g)),
        out_shape=jax.ShapeDtypeStruct((2, micro * length, count * HD), jnp.bfloat16),
        cost_estimate=pl.CostEstimate(flops=0, bytes_accessed=0, transcendentals=0),
        compiler_params=pltpu.CompilerParams(vmem_limit_bytes=VMEM),
        name="attention_grads",
    )(keys, values, queries, grads, places)


def side_by_side(low_ref, high_ref):
    parts = [low_ref[0], high_ref[0], low_ref[1], high_ref[1]]
    return jnp.concatenate(parts, axis=1)


def weight_body(own_ref, other_ref, own_low, own_high, other_low, other_high, out_ref):
    rows = own_ref.shape[1]
    own_d = side_by_side(own_low, own_high)
    other_d = side_by_side(other_low, other_high)
    total = lax.dot_general(own_ref[...], own_d, TN, preferred_element_type=jnp.float32)
    total += lax.dot_general(other_ref[...], other_d, TN, preferred_element_type=jnp.float32)
    most = jnp.maximum(jnp.max(jnp.abs(total), axis=0, keepdims=True), 1e-30)
    power = jnp.ceil(jnp.log2(most * (1.0 / 32000.0)))
    coded = jnp.round(total * jnp.exp2(-power)).astype(jnp.int32)
    out_ref[0, :rows] = coded.astype(jnp.int16)
    tail = jnp.broadcast_to(power.astype(jnp.int32), (PAD, power.shape[1]))
    out_ref[0, rows:] = tail.astype(jnp.int16)


def weight_terms(own, other, own_d, other_d, chunks):
    tokens, width = own.shape
    rows = width // chunks
    columns = 4 * own_d[0].shape[2]
    block = pl.BlockSpec((tokens, rows), lambda k: (0, k))
    whole = pl.BlockSpec(own_d[0].shape, lambda k: (0, 0, 0))
    return pl.pallas_call(
        weight_body,
        grid=(chunks,),
        in_specs=[block, block, whole, whole, whole, whole],
        out_specs=pl.BlockSpec((1, rows + PAD, columns), lambda k: (k, 0, 0)),
        out_shape=jax.ShapeDtypeStruct((chunks, rows + PAD, columns), jnp.int16),
        cost_estimate=pl.CostEstimate(flops=0, bytes_accessed=0, transcendentals=0),
        compiler_params=pltpu.CompilerParams(vmem_limit_bytes=VMEM),
        name="weight_terms",
    )(own, other, *own_d, *other_d)


def branch_body(x_ref, low_ref, high_ref, wk_ref, wv_ref, gain_ref, out_ref, term_ref):
    width = x_ref.shape[1]
    dk = jnp.concatenate([low_ref[0], high_ref[0]], axis=1)
    dv = jnp.concatenate([low_ref[1], high_ref[1]], axis=1)
    dnormed = lax.dot_general(dk, wk_ref[...], NT, preferred_element_type=jnp.float32)
    dnormed += lax.dot_general(dv, wv_ref[...], NT, preferred_element_type=jnp.float32)
    x = x_ref[...].astype(jnp.float32)
    inverse = lax.rsqrt(jnp.sum(x * x, axis=-1, keepdims=True) * (1.0 / width) + EPS)
    unit = x * inverse
    product = dnormed * unit
    term = jnp.sum(product, axis=0, keepdims=True)
    first = pl.program_id(0) == 0

    @pl.when(first)
    def _():
        term_ref[...] = term

    @pl.when(jnp.logical_not(first))
    def _():
        term_ref[...] += term

    gain = gain_ref[...]
    mean = jnp.sum(product * gain, axis=-1, keepdims=True) * (1.0 / width)
    out_ref[...] = inverse * (dnormed * gain - unit * mean)


def branch_terms(x, low, high, wk, wv, gain):
    tokens, width = x.shape
    rows = 128
    half = low.shape[2]
    weight = pl.BlockSpec(wk.shape, lambda i: (0, 0))
    return pl.pallas_call(
        branch_body,
        grid=(tokens // rows,),
        in_specs=[
            pl.BlockSpec((rows, width), lambda i: (i, 0)),
            pl.BlockSpec((2, rows, half), lambda i: (0, i, 0)),
            pl.BlockSpec((2, rows, half), lambda i: (0, i, 0)),
            weight,
            weight,
            pl.BlockSpec((1, width), lambda i: (0, 0)),
        ],
        out_specs=[
            pl.BlockSpec((rows, width), lambda i: (i, 0)),
            pl.BlockSpec((1, width), lambda i: (0, 0)),
        ],
        out_shape=[
            jax.ShapeDtypeStruct((tokens, width), jnp.float32),
            jax.ShapeDtypeStruct((1, width), jnp.float32),
        ],
        cost_estimate=pl.CostEstimate(flops=0, bytes_accessed=0, transcendentals=0),
        compiler_params=pltpu.CompilerParams(vmem_limit_bytes=VMEM),
        name="branch_terms",
    )(x, low, high, wk, wv, gain)


def shards(
    layer_input, queries, attn_grad, top_grad, positions, norm_gain, key_weight, value_weight
):
    _, micro, length, width = layer_input.shape
    tokens = micro * length
    replicas = lax.axis_size("dp")
    chunks = replicas // 2
    rows = width // replicas
    seq_total = micro * replicas
    me = lax.axis_index("dp")
    side = lax.rem(me, 2)
    place = me // 2
    swap = [(i, i ^ 1) for i in range(replicas)]
    wk, wv = key_weight[0], value_weight[0]
    x = layer_input[0].reshape(tokens, width)
    top_full = lax.all_gather(top_grad, "section", axis=2, tiled=True)

    def parity(values, which):
        parts = []
        for k in range(chunks):
            owner = lax.rem(place + k, chunks) * 2 + which
            parts.append(lax.dynamic_slice_in_dim(values, owner * rows, rows, values.ndim - 1))
        return jnp.concatenate(parts, axis=-1)

    x_f = x.astype(jnp.float32)
    inverse = lax.rsqrt(jnp.mean(x_f * x_f, axis=-1, keepdims=True) + EPS)
    normed = (x_f * inverse * norm_gain).astype(jnp.bfloat16)
    normed, given, own = lax.optimization_barrier(
        (normed, parity(normed, 1 - side), parity(normed, side))
    )
    other = lax.ppermute(given, "dp", swap)
    keys = jnp.dot(normed, wk, preferred_element_type=jnp.float32).astype(jnp.bfloat16)
    values = jnp.dot(normed, wv, preferred_element_type=jnp.float32).astype(jnp.bfloat16)

    heads = keys.shape[1] // HD
    half = heads // 2
    places = positions.reshape(micro, 1, length)
    def shift_from(k):
        pairs = []
        for i in range(replicas):
            target = ((i // 2 + k) % chunks) * 2 + i % 2
            pairs.append((i, target))
        return pairs

    grads, theirs = [], []
    for first in (0, half):
        mine = attention_grads(keys, values, queries[0], attn_grad[0], places, first, half)
        grads.append(mine)
        theirs.append(lax.ppermute(mine, "dp", swap))
        keys, mine = lax.optimization_barrier((keys, mine))

    branch, term = branch_terms(x, *grads, wk, wv, norm_gain)
    branch, other, *theirs = lax.optimization_barrier((branch, other, *theirs))
    sections = lax.axis_size("section")
    section = lax.axis_index("section")
    top = top_full.reshape(tokens, width).astype(jnp.float32)
    current = (top + branch).astype(jnp.bfloat16)
    own, current = lax.optimization_barrier((own, current))
    coded = weight_terms(own, other, grads, theirs, chunks)
    pieces = []
    for k in range(1, chunks):
        pieces.append(lax.ppermute(coded[k], "dp", shift_from(k)))
    for s in range(sections - 2, -1, -1):
        came = lax.ppermute(current, "section", [(s + 1, s)])
        if s == sections - 2:
            came, coded = lax.optimization_barrier((came, coded))
        if s == sections - 3:
            came, *pieces = lax.optimization_barrier((came, *pieces))
        added = (came.astype(jnp.float32) + branch).astype(jnp.bfloat16)
        current = jnp.where(section == s, added, current)
    passed = current.reshape(micro, length, width)

    gain_part = parity(term, side) + lax.ppermute(parity(term, 1 - side), "dp", swap)
    gain_share = gain_part[:, :rows]
    for k in range(1, chunks):
        piece = gain_part[:, k * rows : (k + 1) * rows]
        gain_share = gain_share + lax.ppermute(piece, "dp", shift_from(k))
    gain_share = gain_share / seq_total

    total = None
    for piece in [coded[0], *pieces]:
        unit = jnp.exp2(piece[rows : rows + 1].astype(jnp.float32))
        part = piece[:rows].astype(jnp.float32) * unit
        total = part if total is None else total + part
    total = total / seq_total
    wide = keys.shape[1]
    key_share, value_share = total[:, :wide], total[:, wide:]
    return (passed[None], key_share[None], value_share[None], gain_share)


def solution(mesh):
    return jax.shard_map(
        shards,
        mesh=mesh,
        in_specs=(
            P("section", None, "dp", None),
            P("section", None, "dp", None),
            P("section", None, "dp", None),
            P(None, "dp", "section"),
            P(None, "dp"),
            P("section", None),
            P("section", None, None),
            P("section", None, None),
        ),
        out_specs=(
            P("section", None, "dp", None),
            P("section", "dp", None),
            P("section", "dp", None),
            P("section", "dp"),
        ),
        check_vma=False,
    )
```

```python
import functools

import jax
import jax.numpy as jnp
from jax import lax
from jax.experimental import pallas as pl
from jax.experimental.pallas import tpu as pltpu
from jax.sharding import PartitionSpec as P

HD = 128
GRP = 8
EPS = 1e-05
PAD = 16
LOG2E = 1.4426950408889634
VMEM = 50 * 1024 * 1024
NT = (((1,), (1,)), ((), ()))
TN = (((0,), (0,)), ((), ()))


def attention_body(k_ref, v_ref, q_ref, g_ref, pos_ref, out_ref):
    length = k_ref.shape[0]
    scale = HD ** (-0.5)
    keys, values = k_ref[...], v_ref[...]
    key_at = lax.broadcasted_iota(jnp.int32, (length, length), 0)
    query_at = lax.broadcasted_iota(jnp.int32, (length, length), 1)
    distance = query_at - key_at
    allowed = (distance >= 0) & (distance <= pos_ref[0])
    dkeys = jnp.zeros((length, HD), jnp.float32)
    dvalues = jnp.zeros((length, HD), jnp.float32)
    for head in range(GRP):
        columns = slice(head * HD, (head + 1) * HD)
        query, grad = q_ref[0, :, columns], g_ref[0, :, columns]
        scores = lax.dot_general(keys, query, NT, preferred_element_type=jnp.float32)
        scores = jnp.where(allowed, scores, -1e30)
        top = jnp.max(scores, axis=0, keepdims=True)
        raw = jnp.exp2((scores - top) * (scale * LOG2E))
        probs = raw * (1.0 / jnp.sum(raw, axis=0, keepdims=True))
        dprobs = lax.dot_general(values, grad, NT, preferred_element_type=jnp.float32)
        total = jnp.sum(probs * dprobs, axis=0, keepdims=True)
        dscores = (probs * (dprobs - total)).astype(jnp.bfloat16)
        dkeys += jnp.dot(dscores, query, preferred_element_type=jnp.float32)
        dvalues += jnp.dot(probs.astype(jnp.bfloat16), grad, preferred_element_type=jnp.float32)
    out_ref[0] = (dkeys * scale).astype(jnp.bfloat16)
    out_ref[1] = dvalues.astype(jnp.bfloat16)


def attention_grads(keys, values, queries, grads, places, first, count):
    micro, length, _ = queries.shape
    wide = GRP * HD
    return pl.pallas_call(
        attention_body,
        grid=(count, micro),
        in_specs=[
            pl.BlockSpec((length, HD), lambda g, m: (m, first + g)),
            pl.BlockSpec((length, HD), lambda g, m: (m, first + g)),
            pl.BlockSpec((1, length, wide), lambda g, m: (m, 0, first + g)),
            pl.BlockSpec((1, length, wide), lambda g, m: (m, 0, first + g)),
            pl.BlockSpec((1, 1, length), lambda g, m: (m, 0, 0)),
        ],
        out_specs=pl.BlockSpec((2, length, HD), lambda g, m: (0, m, g)),
        out_shape=jax.ShapeDtypeStruct((2, micro * length, count * HD), jnp.bfloat16),
        cost_estimate=pl.CostEstimate(flops=0, bytes_accessed=0, transcendentals=0),
        compiler_params=pltpu.CompilerParams(vmem_limit_bytes=VMEM),
        name="attention_grads",
    )(keys, values, queries, grads, places)


def side_by_side(low_ref, high_ref):
    parts = [low_ref[0], high_ref[0], low_ref[1], high_ref[1]]
    return jnp.concatenate(parts, axis=1)


def weight_body(own_ref, other_ref, own_low, own_high, other_low, other_high, out_ref):
    rows = own_ref.shape[1]
    own_d = side_by_side(own_low, own_high)
    other_d = side_by_side(other_low, other_high)
    total = lax.dot_general(own_ref[...], own_d, TN, preferred_element_type=jnp.float32)
    total += lax.dot_general(other_ref[...], other_d, TN, preferred_element_type=jnp.float32)
    most = jnp.maximum(jnp.max(jnp.abs(total), axis=0, keepdims=True), 1e-30)
    power = jnp.ceil(jnp.log2(most * (1.0 / 32000.0)))
    coded = jnp.round(total * jnp.exp2(-power)).astype(jnp.int32)
    out_ref[0, :rows] = coded.astype(jnp.int16)
    tail = jnp.broadcast_to(power.astype(jnp.int32), (PAD, power.shape[1]))
    out_ref[0, rows:] = tail.astype(jnp.int16)


def weight_terms(own, other, own_d, other_d, chunks):
    tokens, width = own.shape
    rows = width // chunks
    columns = 4 * own_d[0].shape[2]
    block = pl.BlockSpec((tokens, rows), lambda k: (0, k))
    whole = pl.BlockSpec(own_d[0].shape, lambda k: (0, 0, 0))
    return pl.pallas_call(
        weight_body,
        grid=(chunks,),
        in_specs=[block, block, whole, whole, whole, whole],
        out_specs=pl.BlockSpec((1, rows + PAD, columns), lambda k: (k, 0, 0)),
        out_shape=jax.ShapeDtypeStruct((chunks, rows + PAD, columns), jnp.int16),
        cost_estimate=pl.CostEstimate(flops=0, bytes_accessed=0, transcendentals=0),
        compiler_params=pltpu.CompilerParams(vmem_limit_bytes=VMEM),
        name="weight_terms",
    )(own, other, *own_d, *other_d)


def branch_body(x_ref, low_ref, high_ref, wk_ref, wv_ref, gain_ref, out_ref, term_ref):
    width = x_ref.shape[1]
    dk = jnp.concatenate([low_ref[0], high_ref[0]], axis=1)
    dv = jnp.concatenate([low_ref[1], high_ref[1]], axis=1)
    dnormed = lax.dot_general(dk, wk_ref[...], NT, preferred_element_type=jnp.float32)
    dnormed += lax.dot_general(dv, wv_ref[...], NT, preferred_element_type=jnp.float32)
    x = x_ref[...].astype(jnp.float32)
    inverse = lax.rsqrt(jnp.sum(x * x, axis=-1, keepdims=True) * (1.0 / width) + EPS)
    unit = x * inverse
    product = dnormed * unit
    term = jnp.sum(product, axis=0, keepdims=True)
    first = pl.program_id(0) == 0

    @pl.when(first)
    def _():
        term_ref[...] = term

    @pl.when(jnp.logical_not(first))
    def _():
        term_ref[...] += term

    gain = gain_ref[...]
    mean = jnp.sum(product * gain, axis=-1, keepdims=True) * (1.0 / width)
    out_ref[...] = inverse * (dnormed * gain - unit * mean)


def branch_terms(x, low, high, wk, wv, gain):
    tokens, width = x.shape
    rows = 128
    half = low.shape[2]
    weight = pl.BlockSpec(wk.shape, lambda i: (0, 0))
    return pl.pallas_call(
        branch_body,
        grid=(tokens // rows,),
        in_specs=[
            pl.BlockSpec((rows, width), lambda i: (i, 0)),
            pl.BlockSpec((2, rows, half), lambda i: (0, i, 0)),
            pl.BlockSpec((2, rows, half), lambda i: (0, i, 0)),
            weight,
            weight,
            pl.BlockSpec((1, width), lambda i: (0, 0)),
        ],
        out_specs=[
            pl.BlockSpec((rows, width), lambda i: (i, 0)),
            pl.BlockSpec((1, width), lambda i: (0, 0)),
        ],
        out_shape=[
            jax.ShapeDtypeStruct((tokens, width), jnp.float32),
            jax.ShapeDtypeStruct((1, width), jnp.float32),
        ],
        cost_estimate=pl.CostEstimate(flops=0, bytes_accessed=0, transcendentals=0),
        compiler_params=pltpu.CompilerParams(vmem_limit_bytes=VMEM),
        name="branch_terms",
    )(x, low, high, wk, wv, gain)


def shards(
    layer_input, queries, attn_grad, top_grad, positions, norm_gain, key_weight, value_weight
):
    _, micro, length, width = layer_input.shape
    tokens = micro * length
    replicas = lax.axis_size("dp")
    chunks = replicas // 2
    rows = width // replicas
    seq_total = micro * replicas
    me = lax.axis_index("dp")
    side = lax.rem(me, 2)
    place = me // 2
    swap = [(i, i ^ 1) for i in range(replicas)]
    wk, wv = key_weight[0], value_weight[0]
    x = layer_input[0].reshape(tokens, width)
    top_full = lax.all_gather(top_grad, "section", axis=2, tiled=True)

    def parity(values, which):
        parts = []
        for k in range(chunks):
            owner = lax.rem(place + k, chunks) * 2 + which
            parts.append(lax.dynamic_slice_in_dim(values, owner * rows, rows, values.ndim - 1))
        return jnp.concatenate(parts, axis=-1)

    x_f = x.astype(jnp.float32)
    inverse = lax.rsqrt(jnp.mean(x_f * x_f, axis=-1, keepdims=True) + EPS)
    normed = (x_f * inverse * norm_gain).astype(jnp.bfloat16)
    normed, given, own = lax.optimization_barrier(
        (normed, parity(normed, 1 - side), parity(normed, side))
    )
    other = lax.ppermute(given, "dp", swap)
    keys = jnp.dot(normed, wk, preferred_element_type=jnp.float32).astype(jnp.bfloat16)
    values = jnp.dot(normed, wv, preferred_element_type=jnp.float32).astype(jnp.bfloat16)

    heads = keys.shape[1] // HD
    half = heads // 2
    places = positions.reshape(micro, 1, length)
    def shift_from(k):
        pairs = []
        for i in range(replicas):
            target = ((i // 2 + k) % chunks) * 2 + i % 2
            pairs.append((i, target))
        return pairs

    grads, theirs = [], []
    for first in (0, half):
        mine = attention_grads(keys, values, queries[0], attn_grad[0], places, first, half)
        grads.append(mine)
        theirs.append(lax.ppermute(mine, "dp", swap))
        keys, mine = lax.optimization_barrier((keys, mine))

    branch, term = branch_terms(x, *grads, wk, wv, norm_gain)
    branch, other, *theirs = lax.optimization_barrier((branch, other, *theirs))
    sections = lax.axis_size("section")
    section = lax.axis_index("section")
    top = top_full.reshape(tokens, width).astype(jnp.float32)
    current = (top + branch).astype(jnp.bfloat16)
    own, current = lax.optimization_barrier((own, current))
    coded = weight_terms(own, other, grads, theirs, chunks)
    pieces = []
    for k in range(1, chunks):
        pieces.append(lax.ppermute(coded[k], "dp", shift_from(k)))
    gain_part = parity(term, side) + lax.ppermute(parity(term, 1 - side), "dp", swap)
    gain_share = gain_part[:, :rows]
    for k in range(1, chunks):
        piece = gain_part[:, k * rows : (k + 1) * rows]
        gain_share = gain_share + lax.ppermute(piece, "dp", shift_from(k))
    gain_share = gain_share / seq_total
    for s in range(sections - 2, -1, -1):
        came = lax.ppermute(current, "section", [(s + 1, s)])
        if s == sections - 2:
            came, coded = lax.optimization_barrier((came, coded))
        if s == sections - 3:
            came, gain_share, *pieces = lax.optimization_barrier(
                (came, gain_share, *pieces)
            )
        added = (came.astype(jnp.float32) + branch).astype(jnp.bfloat16)
        current = jnp.where(section == s, added, current)
    passed = current.reshape(micro, length, width)

    total = None
    for piece in [coded[0], *pieces]:
        unit = jnp.exp2(piece[rows : rows + 1].astype(jnp.float32))
        part = piece[:rows].astype(jnp.float32) * unit
        total = part if total is None else total + part
    total = total / seq_total
    wide = keys.shape[1]
    key_share, value_share = total[:, :wide], total[:, wide:]
    return (passed[None], key_share[None], value_share[None], gain_share)


def solution(mesh):
    return jax.shard_map(
        shards,
        mesh=mesh,
        in_specs=(
            P("section", None, "dp", None),
            P("section", None, "dp", None),
            P("section", None, "dp", None),
            P(None, "dp", "section"),
            P(None, "dp"),
            P("section", None),
            P("section", None, None),
            P("section", None, None),
        ),
        out_specs=(
            P("section", None, "dp", None),
            P("section", "dp", None),
            P("section", "dp", None),
            P("section", "dp"),
        ),
        check_vma=False,
    )
```
